32 devices in a mesh: prow: 4 (over x, core), pcol: 8 (over z, y).
Axes of the slice: x: 2, y: 2, z: 4, core: 2. Of those that a mesh axis runs over, the one named last changes fastest.
Arguments:
- trailing: float32 [2048, 2048], P('prow', 'pcol'), may hold values from -6 to 6
- panels: float32 [2048, 1024], P('prow', 'pcol'), may hold values from -0.1875 to 0.1875
- diag_inv: float32 [4, 256, 256], replicated, may hold values from -6 to 6
- ancestors: int32 [4, 4], replicated, may hold values from 0 to 7, as said below
- owner_map: int32 [8], replicated, may hold values from 0 to 7, each once
Outputs:
- inv_panel: float32 [2048, 1024], P(('prow', 'pcol'))
- inv_upper: float32 [1024, 2048], P('pcol', 'prow')
- inv_diag: float32 [4, 256, 256], replicated
The draws below stay inside these ranges and needn't reach their ends.
Inputs may be any that keep to these rules, and one draw needn't show every extreme that they name: `ancestors`: each row names 4 distinct blocks; every block is named by exactly two siblings.
All inputs are finite; a program needn't handle non-finite values.
Results may differ from the reference program's by a relative error of at most 0.000071.
Values sent between devices are 32-bit elements; how exact they have to be, the bound alone decides.
A program may use at most 64 MiB of HBM per device.

```python
import jax
import jax.numpy as jnp
from jax import lax

NB = 256
SIBS = 4
NBLK = 8
ROWS = 2048
ANC_SET = 4
PANEL = 1024


def draw_ancestors(key, part):
    base = jax.random.permutation(jax.random.fold_in(key, 17), NBLK).astype(jnp.int32)
    offsets = jnp.arange(ANC_SET, dtype=jnp.int32)
    starts = jnp.arange(SIBS, dtype=jnp.int32) * (NBLK // SIBS)
    places = (starts[:, None] + offsets[None, :]) % NBLK
    return base[places].astype(jnp.int32)


def steps_of(rng, extent, cuts, least, high):
    gain, own = 1.0, jax.random.fold_in(rng, 6)
    for axis_at, blocks in cuts:
        steps = jnp.exp(jax.random.uniform(jax.random.fold_in(own, axis_at), (blocks,), jnp.float32, least / len(cuts), high / len(cuts)))
        gain = gain * jnp.repeat(steps, extent[axis_at] // blocks).reshape([-1 if axis == axis_at else 1 for axis in range(len(extent))])
    return gain


def scatter_about(stream_key, extent, width, reach, pieces=(), kind=jnp.bfloat16):
    loudness = steps_of(stream_key, extent, pieces, -0.22, 0.18) if pieces else 1.0
    result = jax.random.normal(stream_key, extent, jnp.float32) * width * loudness
    return jnp.minimum(jnp.maximum(result, -reach), reach).astype(kind)


def setup_inputs(seed: int = 0) -> dict:
    key_list = jax.random.split(jax.random.key(seed), 6)
    return {
        "trailing": scatter_about(key_list[0], (ROWS, ROWS), 1.0, 6.0, ((0, 4), (1, 8)), jnp.float32),
        "panels": scatter_about(key_list[1], (ROWS, PANEL), (NB * NBLK // 2) ** -0.5, 0.1875, ((0, 4), (1, 8)), jnp.float32),
        "diag_inv": scatter_about(key_list[2], (SIBS, NB, NB), 1.0, 6.0, (), jnp.float32),
        "ancestors": draw_ancestors(jax.random.fold_in(key_list[5], 71), 0),
        "owner_map": jax.random.permutation(key_list[4], NBLK).astype(jnp.int32),
    }


def reference(trailing, panels, diag_inv, ancestors, owner_map):
    nblk = owner_map.shape[0]
    slots = owner_map[ancestors]
    member = jnp.any(slots[:, :, None] == jnp.arange(nblk, dtype=jnp.int32)[None, None, :], axis=1).astype(jnp.float32)
    mask = jnp.repeat(jnp.repeat(member.T, NB, axis=0), NB, axis=1)
    masked = panels * mask
    product = jnp.dot(trailing, masked, precision=lax.Precision.HIGHEST, preferred_element_type=jnp.float32)
    inv_panel = -product * mask
    inv_upper = inv_panel.T
    term = jnp.einsum("rjn,rjm->jnm", masked.reshape(-1, SIBS, NB), inv_panel.reshape(-1, SIBS, NB), precision=lax.Precision.HIGHEST)
    inv_diag = diag_inv - term
    return inv_panel, inv_upper, inv_diag
```

```python
import functools

import jax
import jax.numpy as jnp
from jax import lax
from jax.experimental import pallas as pl
from jax.experimental.pallas import tpu as pltpu
from jax.sharding import PartitionSpec as P

NB = 256
SIBS = 4
SHARE = 2
F32 = jnp.float32
BF16 = jnp.bfloat16


def split(value):
    high = value.astype(BF16)
    return high, (value - high.astype(F32)).astype(BF16)


def dot3(a, b):
    a_high, a_low = a
    b_high, b_low = b
    dot = functools.partial(jnp.dot, preferred_element_type=F32)
    return dot(a_high, b_high) + (dot(a_high, b_low) + dot(a_low, b_high))


def kernel(
    R, C, an, om, t_ref, p_ref, panel_ref, upper_ref, diag_ref,
    pg, grp, mt, b_ref, y, yr, zr, stage, u, d_ref, rr,
    a1_s, a1_r, g_s, g_r, a2_s, a2_r, a2f_s, a2f_r, y_s, y_r, z_s, z_r,
    u_s, u_r, d_s, d_r, ez_s, ez_r, ey_s, ey_r, ex_s, ex_r, ec_s, ec_r,
):
    r = lax.axis_index("prow")
    c = lax.axis_index("pcol")
    rows, cols = t_ref.shape
    width = p_ref.shape[1]
    ratio = rows // cols
    quarter = cols // R
    part = rows // C
    group = NB // width
    half = C // 2
    pairs = R // 2
    chunk = NB // R
    par = lax.rem(c, 2)
    other_c = c + 1 - 2 * par
    rpar = lax.rem(r, 2)
    other_r = r + 1 - 2 * rpar
    sends = []

    def copy(src, dst, ssem, rsem, to_r, to_c):
        return pltpu.make_async_remote_copy(
            src_ref=src, dst_ref=dst, send_sem=ssem, recv_sem=rsem,
            device_id=(to_r, to_c), device_id_type=pl.DeviceIdType.MESH,
        )

    def send(*args):
        op = copy(*args)
        op.start()
        sends.append(op)

    def arrived(dst, ssem, rsem):
        copy(dst, dst, ssem, rsem, other_r, c).wait_recv()

    def same_parity(index, count, step):
        return lax.rem(index // 2 + step, count) * 2 + lax.rem(index, 2)

    own = []
    for step in [*range(1, R), 0]:
        k = lax.rem(r + step, R)
        for b in range(ratio):
            dest = r * ratio + b
            piece = p_ref.at[pl.ds(pl.multiple_of(b * cols + k * quarter, quarter), quarter)]
            args = (piece, pg.at[k, c], a1_s.at[b, step], a1_r.at[c], k, dest)
            if step:
                send(*args)
            else:
                own.append((dest, args))
    for dest, args in own:
        @pl.when(dest != c)
        def _():
            copy(*args).start()

        @pl.when(dest == c)
        def _():
            pg[r, c] = args[0][...]

    base = (c // group) * group
    member = c - base
    for step in range(1, group):
        to = base + lax.rem(member + step, group)
        send(p_ref, grp.at[member], g_s.at[step - 1], g_r.at[step - 1], r, to)
    grp[member] = p_ref[...]

    slots = [[om[an[j, a]] for a in range(an.shape[1])] for j in range(SIBS)]

    def members(s):
        found = []
        for j in range(SIBS):
            flag = jnp.int32(0)
            for slot in slots[j]:
                flag = flag | jnp.where(slot == s, 1, 0).astype(jnp.int32)
            found.append(flag)
        return found

    def places(s):
        flags, before = members(s), jnp.int32(0)
        out = [[] for _ in range(SHARE)]
        for flag in flags:
            for k in range(SHARE):
                out[k].append((flag * jnp.where(before == k, 1, 0).astype(jnp.int32)).astype(F32))
            before = before + flag
        return out

    row_blocks = rows // NB
    row_places = [places(r * row_blocks + b) for b in range(row_blocks)]
    my_place = places((r * rows + c * part) // NB)
    col_flags = [flag.astype(F32) for flag in members(c)]

    root = c // ratio
    for step in range(SIBS):
        j = lax.rem(c // group + step, SIBS)
        for i in range(group):
            source = j * group + i
            @pl.when(jnp.logical_not((root == r) & (source == c)))
            def _():
                arrived(pg.at[r, source], a1_s.at[0, 0], a1_r.at[source])
        block = pg.at[r, pl.ds(j * group, group)]
        for to in range(1, pairs):
            send(block, block, a2_s.at[to, step], a2_r.at[to, j], same_parity(r, pairs, to), c)
        send(block, block, a2_s.at[0, step], a2_r.at[0, j], other_r, c)
    for step in range(SIBS):
        for to in range(1, pairs):
            j = lax.rem(c // group + step, SIBS)
            source = same_parity(r, pairs, pairs - to)
            block = pg.at[source, pl.ds(j * group, group)]
            arrived(block, a2_s.at[to, step], a2_r.at[to, j])
            send(block, block, a2f_s.at[to - 1, step], a2f_r.at[to - 1, j], other_r, c)
    for j in range(SIBS):
        arrived(pg.at[other_r, pl.ds(j * group, group)], a2_s.at[0, j], a2_r.at[0, j])
        for to in range(1, pairs):
            source = same_parity(other_r, pairs, pairs - to)
            block = pg.at[source, pl.ds(j * group, group)]
            arrived(block, a2f_s.at[to - 1, j], a2f_r.at[to - 1, j])

    for s in range(row_blocks):
        for k in range(SHARE):
            scale = [row_places[s][k][j] * col_flags[j] for j in range(SIBS)]
            for q in range(R):
                for i in range(group):
                    total = scale[0] * pg[q, i]
                    for j in range(1, SIBS):
                        total = total + scale[j] * pg[q, j * group + i]
                    b_ref[s, q * quarter:(q + 1) * quarter,
                          k * NB + i * width:k * NB + (i + 1) * width] = total
        y[s * NB:(s + 1) * NB, :] = dot3(split(t_ref[s * NB:(s + 1) * NB, :]), split(b_ref[s]))
        for i in range(s * NB // (2 * part), (s + 1) * NB // (2 * part)):
            piece = y.at[pl.ds(pl.multiple_of((2 * i + 1 - par) * part, part), part)]
            send(piece, yr.at[i], y_s.at[i], y_r.at[i], r, other_c)

    for step in [*range(1, half), 0]:
        i = lax.rem(c // 2 + step, half)
        place = pl.ds(pl.multiple_of((2 * i + par) * part, part), part)
        arrived(yr.at[i], y_s.at[i], y_r.at[i])
        y[place, :] = y[place, :] + yr[i]
        if step:
            send(y.at[place], zr.at[step - 1], z_s.at[step - 1], z_r.at[step - 1], r, 2 * i + par)

    for step in range(1, group):
        source = base + lax.rem(member + group - step, group)
        arrived(grp.at[source - base], g_s.at[step - 1], g_r.at[step - 1])
    for i in range(group):
        mt[i * width:(i + 1) * width, :] = grp[i].T
    mt_split = split(mt[...])

    total = y[pl.ds(pl.multiple_of(c * part, part), part), :]
    for step in range(1, half):
        arrived(zr.at[step - 1], z_s.at[step - 1], z_r.at[step - 1])
        total = total + zr[step - 1]
    for j in range(SIBS):
        block = -(my_place[0][j] * total[:, :NB] + my_place[1][j] * total[:, NB:])
        panel_ref[:, j * NB:(j + 1) * NB] = block
        for i in range(group):
            stage[j * group + i] = block[:, i * width:(i + 1) * width]

    for step in range(1, C):
        to = lax.rem(c + step, C)
        send(stage.at[to], u.at[c], u_s.at[step - 1], u_r.at[step - 1], r, to)
    u[c] = stage[c]
    for step in range(1, C):
        source = lax.rem(c + C - step, C)
        arrived(u.at[source], u_s.at[step - 1], u_r.at[step - 1])
    x = u[...].reshape(rows, width)
    upper_ref[...] = x.T

    d_ref[...] = dot3(mt_split, split(x))
    for step in range(1, R):
        to = lax.rem(r + step, R)
        piece = d_ref.at[pl.ds(pl.multiple_of(to * chunk, chunk), chunk)]
        send(piece, rr.at[step - 1], d_s.at[step - 1], d_r.at[step - 1], to, c)
    total = d_ref[pl.ds(pl.multiple_of(r * chunk, chunk), chunk), :]
    for step in range(1, R):
        arrived(rr.at[step - 1], d_s.at[step - 1], d_r.at[step - 1])
        total = total + rr[step - 1]
    place = c // 2
    diag_ref[par, r, place] = total
    mine = diag_ref.at[par, r, place]
    for step in range(1, half):
        to = lax.rem(place + step, half)
        send(mine, mine, ez_s.at[step - 1], ez_r.at[step - 1], r, 2 * to + par)
    for step in range(1, half):
        source = lax.rem(place + half - step, half)
        arrived(diag_ref.at[par, r, source], ez_s.at[step - 1], ez_r.at[step - 1])

    def spread(which, block):
        for to in range(1, pairs):
            send(block, block, ex_s.at[which, to], ex_r.at[which, to], same_parity(r, pairs, to), c)
        send(block, block, ec_s.at[which, 0], ec_r.at[which, 0], other_r, c)

    block = diag_ref.at[par, r]
    send(block, block, ey_s.at[0], ey_r.at[0], r, other_c)
    spread(0, block)
    block = diag_ref.at[1 - par, r]
    arrived(block, ey_s.at[0], ey_r.at[0])
    spread(1, block)
    for which in range(2):
        side = par if which == 0 else 1 - par
        for to in range(1, pairs):
            block = diag_ref.at[side, same_parity(r, pairs, pairs - to)]
            arrived(block, ex_s.at[which, to], ex_r.at[which, to])
            send(block, block, ec_s.at[which, to], ec_r.at[which, to], other_r, c)
    for which in range(2):
        side = par if which == 0 else 1 - par
        for to in range(pairs):
            block = diag_ref.at[side, same_parity(other_r, pairs, (pairs - to) % pairs)]
            arrived(block, ec_s.at[which, to], ec_r.at[which, to])

    for op in sends:
        op.wait_send()
    for dest, args in own:
        @pl.when(dest != c)
        def _():
            copy(*args).wait_send()


def shards(R, C, trailing, panels, diag_inv, ancestors, owner_map):
    rows, cols = trailing.shape
    width = panels.shape[1]
    ratio = rows // cols
    part = rows // C
    group = NB // width
    half = C // 2
    pairs = R // 2
    chunk = NB // R
    wide = SHARE * NB
    dma = pltpu.SemaphoreType.DMA
    sems = []
    for shape in (
        (ratio, R), (C,), (max(group - 1, 1),), (max(group - 1, 1),),
        (pairs, SIBS), (pairs, SIBS), (max(pairs - 1, 1), SIBS), (max(pairs - 1, 1), SIBS),
        (half,), (half,), (half - 1,), (half - 1,), (C - 1,), (C - 1,),
        (R - 1,), (R - 1,), (half - 1,), (half - 1,), (1,), (1,),
        (2, pairs), (2, pairs), (2, pairs), (2, pairs),
    ):
        sems.append(dma(shape))
    vmem = pl.BlockSpec(memory_space=pltpu.VMEM)
    smem = pl.BlockSpec(memory_space=pltpu.SMEM)
    inv_panel, inv_upper, term = pl.pallas_call(
        functools.partial(kernel, R, C),
        out_shape=(
            jax.ShapeDtypeStruct((part, SIBS * NB), F32),
            jax.ShapeDtypeStruct((width, rows), F32),
            jax.ShapeDtypeStruct((2, R, half, chunk, width), F32),
        ),
        in_specs=[smem, smem, vmem, vmem],
        out_specs=(vmem, vmem, vmem),
        scratch_shapes=[
            pltpu.VMEM((R, C, cols // R, width), F32),
            pltpu.VMEM((group, rows, width), F32),
            pltpu.VMEM((NB, rows), F32),
            pltpu.VMEM((rows // NB, cols, wide), F32),
            pltpu.VMEM((rows, wide), F32),
            pltpu.VMEM((half, part, wide), F32),
            pltpu.VMEM((half - 1, part, wide), F32),
            pltpu.VMEM((C, part, width), F32),
            pltpu.VMEM((C, part, width), F32),
            pltpu.VMEM((NB, width), F32),
            pltpu.VMEM((R - 1, chunk, width), F32),
            *sems,
        ],
        compiler_params=pltpu.CompilerParams(
            has_side_effects=True, vmem_limit_bytes=40 * 1024 * 1024
        ),
    )(ancestors, owner_map, trailing, panels)
    term = term.reshape(2, R, SIBS, group // 2, chunk, width)
    term = term.transpose(2, 1, 4, 3, 0, 5).reshape(SIBS, NB, NB)
    return inv_panel, inv_upper, diag_inv - term


def solution(mesh):
    placed = (P("prow", "pcol"), P("prow", "pcol"), P(), P(), P())
    return jax.shard_map(
        functools.partial(shards, mesh.shape["prow"], mesh.shape["pcol"]),
        mesh=mesh,
        in_specs=placed,
        out_specs=(P(("prow", "pcol"), None), P("pcol", "prow"), P()),
        check_vma=False,
    )
```

```python
import functools

import jax
import jax.numpy as jnp
from jax import lax
from jax.experimental import pallas as pl
from jax.experimental.pallas import tpu as pltpu
from jax.sharding import PartitionSpec as P

NB = 256
SIBS = 4
SHARE = 2
F32 = jnp.float32
BF16 = jnp.bfloat16


def split(value):
    high = value.astype(BF16)
    return high, (value - high.astype(F32)).astype(BF16)


def dot3(a, b):
    a_high, a_low = a
    b_high, b_low = b
    dot = functools.partial(jnp.dot, preferred_element_type=F32)
    return dot(a_high, b_high) + (dot(a_high, b_low) + dot(a_low, b_high))


def kernel(
    R, C, an_hbm, om_hbm, t_hbm, p_ref, inv_hbm, panel_ref, upper_ref, diag_ref,
    an, om, t_ref, inv_ref, t_high, t_low,
    pg, grp, mt, b_ref, y, yr, zr, stage, u, d_ref, rr, eg,
    load, a1_s, a1_r, g_s, g_r, a2_s, a2_r, a2f_s, a2f_r, y_s, y_r, z_s, z_r,
    u_s, u_r, d_s, d_r, ez_s, ez_r, ey_s, ey_r, ex_s, ex_r, ec_s, ec_r,
):
    r = lax.axis_index("prow")
    c = lax.axis_index("pcol")
    rows, cols = t_ref.shape
    width = p_ref.shape[1]
    ratio = rows // cols
    quarter = cols // R
    part = rows // C
    group = NB // width
    half = C // 2
    pairs = R // 2
    chunk = NB // R
    par = lax.rem(c, 2)
    other_c = c + 1 - 2 * par
    rpar = lax.rem(r, 2)
    other_r = r + 1 - 2 * rpar
    sends = []

    def copy(src, dst, ssem, rsem, to_r, to_c):
        return pltpu.make_async_remote_copy(
            src_ref=src, dst_ref=dst, send_sem=ssem, recv_sem=rsem,
            device_id=(to_r, to_c), device_id_type=pl.DeviceIdType.MESH,
        )

    def send(*args):
        op = copy(*args)
        op.start()
        sends.append(op)

    def arrived(dst, ssem, rsem):
        copy(dst, dst, ssem, rsem, other_r, c).wait_recv()

    def flip(index, bits):
        bit = 1
        out = index
        while bit <= bits:
            if bits & bit:
                out = out + bit * (1 - 2 * lax.rem(index // bit, 2))
            bit *= 2
        return out

    def same_parity(index, count, step):
        return lax.rem(index // 2 + step, count) * 2 + lax.rem(index, 2)

    loads = [
        pltpu.make_async_copy(src, dst, load.at[n])
        for n, (src, dst) in enumerate(
            ((p_ref, grp.at[lax.rem(c, group)]), (an_hbm, an), (om_hbm, om), (t_hbm, t_ref),
             (inv_hbm, inv_ref))
        )
    ]
    for op in loads:
        op.start()

    own = []
    for step in [*range(1, R), 0]:
        k = lax.rem(r + step, R)
        for b in range(ratio):
            dest = r * ratio + b
            span = pl.ds(pl.multiple_of(b * cols + k * quarter, quarter), quarter)
            piece = p_ref.at[span]
            args = (piece, pg.at[k, c], a1_s.at[b, step], a1_r.at[c], k, dest)
            if step:
                send(*args)
            else:
                own.append((dest, args, span))
    base = (c // group) * group
    member = c - base
    for dest, args, span in own:
        @pl.when(dest != c)
        def _():
            copy(*args).start()
    loads[0].wait()
    for dest, args, span in own:
        @pl.when(dest == c)
        def _():
            pg[r, c] = grp[member, span, :]
    for op in loads[1:4]:
        op.wait()
    t_high[...], t_low[...] = split(t_ref[...])

    slots = [[om[an[j, a]] for a in range(an.shape[1])] for j in range(SIBS)]

    def members(s):
        found = []
        for j in range(SIBS):
            flag = jnp.int32(0)
            for slot in slots[j]:
                flag = flag | jnp.where(slot == s, 1, 0).astype(jnp.int32)
            found.append(flag)
        return found

    def places(s):
        flags, before = members(s), jnp.int32(0)
        out = [[] for _ in range(SHARE)]
        for flag in flags:
            for k in range(SHARE):
                out[k].append((flag * jnp.where(before == k, 1, 0).astype(jnp.int32)).astype(F32))
            before = before + flag
        return out

    row_blocks = rows // NB
    row_places = [places(r * row_blocks + b) for b in range(row_blocks)]
    my_place = places((r * rows + c * part) // NB)
    col_flags = [flag.astype(F32) for flag in members(c)]

    root = c // ratio
    for step in range(SIBS):
        j = lax.rem(c // group + step, SIBS)
        for i in range(group):
            source = j * group + i
            @pl.when(jnp.logical_not((root == r) & (source == c)))
            def _():
                arrived(pg.at[r, source], a1_s.at[0, 0], a1_r.at[source])
        block = pg.at[r, pl.ds(j * group, group)]
        for to in range(1, pairs):
            send(block, block, a2_s.at[to, step], a2_r.at[to, j], same_parity(r, pairs, to), c)
        send(block, block, a2_s.at[0, step], a2_r.at[0, j], other_r, c)
    for step in range(1, group):
        to = base + lax.rem(member + step, group)
        send(p_ref, grp.at[member], g_s.at[step - 1], g_r.at[step - 1], r, to)
    for step in range(SIBS):
        for to in range(1, pairs):
            j = lax.rem(c // group + step, SIBS)
            source = same_parity(r, pairs, pairs - to)
            block = pg.at[source, pl.ds(j * group, group)]
            arrived(block, a2_s.at[to, step], a2_r.at[to, j])
            send(block, block, a2f_s.at[to - 1, step], a2f_r.at[to - 1, j], other_r, c)
    for j in range(SIBS):
        arrived(pg.at[other_r, pl.ds(j * group, group)], a2_s.at[0, j], a2_r.at[0, j])
        for to in range(1, pairs):
            source = same_parity(other_r, pairs, pairs - to)
            block = pg.at[source, pl.ds(j * group, group)]
            arrived(block, a2f_s.at[to - 1, j], a2f_r.at[to - 1, j])

    for s in range(row_blocks):
        for k in range(SHARE):
            scale = [row_places[s][k][j] * col_flags[j] for j in range(SIBS)]
            for q in range(R):
                for i in range(group):
                    total = scale[0] * pg[q, i]
                    for j in range(1, SIBS):
                        total = total + scale[j] * pg[q, j * group + i]
                    b_ref[s, q * quarter:(q + 1) * quarter,
                          k * NB + i * width:k * NB + (i + 1) * width] = total
        here = slice(s * NB, (s + 1) * NB)
        y[here, :] = dot3((t_high[here, :], t_low[here, :]), split(b_ref[s]))

    order = [flip(c // 2, step) for step in (*range(half - 1, 0, -1), 0)]
    for i in order:
        piece = y.at[pl.ds(pl.multiple_of((2 * i + 1 - par) * part, part), part)]
        send(piece, yr.at[i], y_s.at[i], y_r.at[i], r, other_c)
    for step, i in zip((*range(half - 1, 0, -1), 0), order):
        place = pl.ds(pl.multiple_of((2 * i + par) * part, part), part)
        arrived(yr.at[i], y_s.at[i], y_r.at[i])
        y[place, :] = y[place, :] + yr[i]
        if step:
            send(y.at[place], zr.at[step - 1], z_s.at[step - 1], z_r.at[step - 1], r, 2 * i + par)

    for step in range(1, group):
        source = base + lax.rem(member + group - step, group)
        arrived(grp.at[source - base], g_s.at[step - 1], g_r.at[step - 1])
    for i in range(group):
        mt[i * width:(i + 1) * width, :] = grp[i].T
    mt_split = split(mt[...])

    total = y[pl.ds(pl.multiple_of(c * part, part), part), :]
    for step in range(1, half):
        arrived(zr.at[step - 1], z_s.at[step - 1], z_r.at[step - 1])
        total = total + zr[step - 1]
    for j in range(SIBS):
        block = -(my_place[0][j] * total[:, :NB] + my_place[1][j] * total[:, NB:])
        panel_ref[:, j * NB:(j + 1) * NB] = block
        for i in range(group):
            stage[j * group + i] = block[:, i * width:(i + 1) * width]

    for step in range(1, C):
        to = lax.rem(c + step, C)
        send(stage.at[to], u.at[c], u_s.at[step - 1], u_r.at[step - 1], r, to)
    u[c] = stage[c]
    for step in range(1, C):
        source = lax.rem(c + C - step, C)
        arrived(u.at[source], u_s.at[step - 1], u_r.at[step - 1])
    x = u[...].reshape(rows, width)
    upper_ref[...] = x.T

    d_ref[...] = dot3(mt_split, split(x))
    for step in range(1, R):
        to = lax.rem(r + step, R)
        piece = d_ref.at[pl.ds(pl.multiple_of(to * chunk, chunk), chunk)]
        send(piece, rr.at[step - 1], d_s.at[step - 1], d_r.at[step - 1], to, c)
    total = d_ref[pl.ds(pl.multiple_of(r * chunk, chunk), chunk), :]
    for step in range(1, R):
        arrived(rr.at[step - 1], d_s.at[step - 1], d_r.at[step - 1])
        total = total + rr[step - 1]
    place = c // 2
    eg[par, r, place] = total

    def spread(which, step, side, at, over_pair):
        block = eg.at[side, r, at]
        if over_pair:
            send(block, block, ey_s.at[step], ey_r.at[step], r, other_c)
        for to in range(1, pairs):
            send(block, block, ex_s.at[which, to, step], ex_r.at[which, to, step],
                 same_parity(r, pairs, to), c)
        send(block, block, ec_s.at[which, 0, step], ec_r.at[which, 0, step], other_r, c)

    def onward(which, step, side, at):
        for to in range(1, pairs):
            block = eg.at[side, same_parity(r, pairs, pairs - to), at]
            arrived(block, ex_s.at[which, to, step], ex_r.at[which, to, step])
            send(block, block, ec_s.at[which, to, step], ec_r.at[which, to, step], other_r, c)

    mine = eg.at[par, r, place]
    for step in range(half - 1, 0, -1):
        to = flip(place, step)
        send(mine, mine, ez_s.at[step - 1], ez_r.at[step - 1], r, 2 * to + par)
    spread(0, 0, par, place, True)
    events = [(0, 1), (1, 0)]
    for step in range(2, half):
        events += [(0, step), (1, step - 1)]
    events.append((1, half - 1))
    before = (0, 0)
    for which, step in events:
        at = flip(place, step)
        if which == 0:
            arrived(eg.at[par, r, at], ez_s.at[step - 1], ez_r.at[step - 1])
            spread(0, step, par, at, True)
        else:
            arrived(eg.at[1 - par, r, at], ey_s.at[step], ey_r.at[step])
            spread(1, step, 1 - par, at, False)
        side = par if before[0] == 0 else 1 - par
        onward(*before, side, flip(place, before[1]))
        before = (which, step)
    onward(*before, par if before[0] == 0 else 1 - par, flip(place, before[1]))
    loads[4].wait()
    for which in range(2):
        side = par if which == 0 else 1 - par
        for step in range(half):
            for to in range(pairs):
                block = eg.at[side, same_parity(other_r, pairs, (pairs - to) % pairs), flip(place, step)]
                arrived(block, ec_s.at[which, to, step], ec_r.at[which, to, step])
    for column in range(C):
        j, i = column // group, column % group
        lanes = slice(i * width, (i + 1) * width)
        for k in range(R):
            span = slice(k * chunk, (k + 1) * chunk)
            diag_ref[j, span, lanes] = inv_ref[j, span, lanes] - eg[column % 2, k, column // 2]

    for op in sends:
        op.wait_send()
    for dest, args, span in own:
        @pl.when(dest != c)
        def _():
            copy(*args).wait_send()


def shards(R, C, trailing, panels, diag_inv, ancestors, owner_map):
    rows, cols = trailing.shape
    width = panels.shape[1]
    ratio = rows // cols
    part = rows // C
    group = NB // width
    half = C // 2
    pairs = R // 2
    chunk = NB // R
    wide = SHARE * NB
    dma = pltpu.SemaphoreType.DMA
    sems = [dma((5,))]
    for shape in (
        (ratio, R), (C,), (max(group - 1, 1),), (max(group - 1, 1),),
        (pairs, SIBS), (pairs, SIBS), (max(pairs - 1, 1), SIBS), (max(pairs - 1, 1), SIBS),
        (half,), (half,), (half - 1,), (half - 1,), (C - 1,), (C - 1,),
        (R - 1,), (R - 1,), (half - 1,), (half - 1,), (half,), (half,),
        (2, pairs, half), (2, pairs, half), (2, pairs, half), (2, pairs, half),
    ):
        sems.append(dma(shape))
    vmem = pl.BlockSpec(memory_space=pltpu.VMEM)
    anywhere = pl.BlockSpec(memory_space=pl.ANY)
    return pl.pallas_call(
        functools.partial(kernel, R, C),
        out_shape=(
            jax.ShapeDtypeStruct((part, SIBS * NB), F32),
            jax.ShapeDtypeStruct((width, rows), F32),
            jax.ShapeDtypeStruct(diag_inv.shape, F32),
        ),
        in_specs=[anywhere] * 5,
        out_specs=(vmem, vmem, vmem),
        scratch_shapes=[
            pltpu.SMEM(ancestors.shape, jnp.int32),
            pltpu.SMEM(owner_map.shape, jnp.int32),
            pltpu.VMEM(trailing.shape, F32),
            pltpu.VMEM(diag_inv.shape, F32),
            pltpu.VMEM(trailing.shape, BF16),
            pltpu.VMEM(trailing.shape, BF16),
            pltpu.VMEM((R, C, cols // R, width), F32),
            pltpu.VMEM((group, rows, width), F32),
            pltpu.VMEM((NB, rows), F32),
            pltpu.VMEM((rows // NB, cols, wide), F32),
            pltpu.VMEM((rows, wide), F32),
            pltpu.VMEM((half, part, wide), F32),
            pltpu.VMEM((half - 1, part, wide), F32),
            pltpu.VMEM((C, part, width), F32),
            pltpu.VMEM((C, part, width), F32),
            pltpu.VMEM((NB, width), F32),
            pltpu.VMEM((R - 1, chunk, width), F32),
            pltpu.VMEM((2, R, half, chunk, width), F32),
            *sems,
        ],
        compiler_params=pltpu.CompilerParams(
            has_side_effects=True, vmem_limit_bytes=56 * 1024 * 1024
        ),
    )(ancestors, owner_map, trailing, panels, diag_inv)


def solution(mesh):
    placed = (P("prow", "pcol"), P("prow", "pcol"), P(), P(), P())
    return jax.shard_map(
        functools.partial(shards, mesh.shape["prow"], mesh.shape["pcol"]),
        mesh=mesh,
        in_specs=placed,
        out_specs=(P(("prow", "pcol"), None), P("pcol", "prow"), P()),
        check_vma=False,
    )
```

```python
import functools

import jax
import jax.numpy as jnp
from jax import lax
from jax.experimental import pallas as pl
from jax.experimental.pallas import tpu as pltpu
from jax.sharding import PartitionSpec as P

NB = 256
SIBS = 4
SHARE = 2
F32 = jnp.float32
BF16 = jnp.bfloat16


def split(value):
    high = value.astype(BF16)
    return high, (value - high.astype(F32)).astype(BF16)


def dot3(a, b):
    a_high, a_low = a
    b_high, b_low = b
    dot = functools.partial(jnp.dot, preferred_element_type=F32)
    return dot(a_high, b_high) + (dot(a_high, b_low) + dot(a_low, b_high))


def kernel(
    R, C, an_hbm, om_hbm, t_hbm, p_ref, inv_hbm, panel_ref, upper_ref, diag_ref,
    an, om, t_ref, inv_ref, t_high, t_low,
    pg, grp, mt, b_ref, y, yr, zr, stage, u, d_ref, rr, eg,
    load, a1_s, a1_r, g_s, g_r, a2_s, a2_r, a2f_s, a2f_r, y_s, y_r, z_s, z_r,
    u_s, u_r, d_s, d_r, ez_s, ez_r, ey_s, ey_r, ex_s, ex_r, ec_s, ec_r,
):
    r = lax.axis_index("prow")
    c = lax.axis_index("pcol")
    rows, cols = t_ref.shape
    width = p_ref.shape[1]
    ratio = rows // cols
    quarter = cols // R
    part = rows // C
    group = NB // width
    half = C // 2
    pairs = R // 2
    chunk = NB // R
    par = lax.rem(c, 2)
    other_c = c + 1 - 2 * par
    rpar = lax.rem(r, 2)
    other_r = r + 1 - 2 * rpar
    sends = []

    def copy(src, dst, ssem, rsem, to_r, to_c):
        return pltpu.make_async_remote_copy(
            src_ref=src, dst_ref=dst, send_sem=ssem, recv_sem=rsem,
            device_id=(to_r, to_c), device_id_type=pl.DeviceIdType.MESH,
        )

    def send(*args):
        op = copy(*args)
        op.start()
        sends.append(op)

    def arrived(dst, ssem, rsem):
        copy(dst, dst, ssem, rsem, other_r, c).wait_recv()

    def flip(index, bits):
        bit = 1
        out = index
        while bit <= bits:
            if bits & bit:
                out = out + bit * (1 - 2 * lax.rem(index // bit, 2))
            bit *= 2
        return out

    def same_parity(index, count, step):
        return lax.rem(index // 2 + step, count) * 2 + lax.rem(index, 2)

    loads = [
        pltpu.make_async_copy(src, dst, load.at[n])
        for n, (src, dst) in enumerate(
            ((p_ref, grp.at[lax.rem(c, group)]), (an_hbm, an), (om_hbm, om), (t_hbm, t_ref),
             (inv_hbm, inv_ref))
        )
    ]
    for op in loads:
        op.start()

    barrier = pltpu.get_barrier_semaphore()

    @pl.loop(1, R * C)
    def _(step):
        peer = lax.rem(r * C + c + step, R * C)
        pl.semaphore_signal(
            barrier, inc=1, device_id=(peer // C, lax.rem(peer, C)),
            device_id_type=pl.DeviceIdType.MESH,
        )

    for op in loads[:4]:
        op.wait()
    t_high[...], t_low[...] = split(t_ref[...])
    pl.semaphore_wait(barrier, R * C - 1)

    own = []
    for step in [*range(1, R), 0]:
        k = lax.rem(r + step, R)
        for b in range(ratio):
            dest = r * ratio + b
            span = pl.ds(pl.multiple_of(b * cols + k * quarter, quarter), quarter)
            piece = p_ref.at[span]
            args = (piece, pg.at[k, c], a1_s.at[b, step], a1_r.at[c], k, dest)
            if step:
                send(*args)
            else:
                own.append((dest, args, span))
    base = (c // group) * group
    member = c - base
    for dest, args, span in own:
        @pl.when(dest != c)
        def _():
            copy(*args).start()
    for dest, args, span in own:
        @pl.when(dest == c)
        def _():
            pg[r, c] = grp[member, span, :]

    slots = [[om[an[j, a]] for a in range(an.shape[1])] for j in range(SIBS)]

    def members(s):
        found = []
        for j in range(SIBS):
            flag = jnp.int32(0)
            for slot in slots[j]:
                flag = flag | jnp.where(slot == s, 1, 0).astype(jnp.int32)
            found.append(flag)
        return found

    def places(s):
        flags, before = members(s), jnp.int32(0)
        out = [[] for _ in range(SHARE)]
        for flag in flags:
            for k in range(SHARE):
                out[k].append((flag * jnp.where(before == k, 1, 0).astype(jnp.int32)).astype(F32))
            before = before + flag
        return out

    row_blocks = rows // NB
    first = (c // 2) // (half // row_blocks)
    blocks = [flip(first, n) for n in range(row_blocks - 1, -1, -1)]
    row_places = [places(r * row_blocks + b) for b in blocks]
    my_place = places((r * rows + c * part) // NB)
    col_flags = [flag.astype(F32) for flag in members(c)]

    root = c // ratio
    for step in range(SIBS):
        j = lax.rem(c // group + step, SIBS)
        for i in range(group):
            source = j * group + i
            @pl.when(jnp.logical_not((root == r) & (source == c)))
            def _():
                arrived(pg.at[r, source], a1_s.at[0, 0], a1_r.at[source])
        block = pg.at[r, pl.ds(j * group, group)]
        for to in range(1, pairs):
            send(block, block, a2_s.at[to, step], a2_r.at[to, j], same_parity(r, pairs, to), c)
        send(block, block, a2_s.at[0, step], a2_r.at[0, j], other_r, c)
    for step in range(1, group):
        to = base + lax.rem(member + step, group)
        send(p_ref, grp.at[member], g_s.at[step - 1], g_r.at[step - 1], r, to)
    for step in range(SIBS):
        for to in range(1, pairs):
            j = lax.rem(c // group + step, SIBS)
            source = same_parity(r, pairs, pairs - to)
            block = pg.at[source, pl.ds(j * group, group)]
            arrived(block, a2_s.at[to, step], a2_r.at[to, j])
            send(block, block, a2f_s.at[to - 1, step], a2f_r.at[to - 1, j], other_r, c)
    for j in range(SIBS):
        arrived(pg.at[other_r, pl.ds(j * group, group)], a2_s.at[0, j], a2_r.at[0, j])
        for to in range(1, pairs):
            source = same_parity(other_r, pairs, pairs - to)
            block = pg.at[source, pl.ds(j * group, group)]
            arrived(block, a2f_s.at[to - 1, j], a2f_r.at[to - 1, j])

    order = [flip(c // 2, step) for step in (*range(half - 1, 0, -1), 0)]
    for s in range(row_blocks):
        for k in range(SHARE):
            scale = [row_places[s][k][j] * col_flags[j] for j in range(SIBS)]
            for q in range(R):
                for i in range(group):
                    total = scale[0] * pg[q, i]
                    for j in range(1, SIBS):
                        total = total + scale[j] * pg[q, j * group + i]
                    b_ref[s, q * quarter:(q + 1) * quarter,
                          k * NB + i * width:k * NB + (i + 1) * width] = total
        here = pl.ds(pl.multiple_of(blocks[s] * NB, NB), NB)
        y[here, :] = dot3((t_high[here, :], t_low[here, :]), split(b_ref[s]))
        each = half // row_blocks
        for i in order[s * each:(s + 1) * each]:
            piece = y.at[pl.ds(pl.multiple_of((2 * i + 1 - par) * part, part), part)]
            send(piece, yr.at[i], y_s.at[i], y_r.at[i], r, other_c)
    for step, i in zip((*range(half - 1, 0, -1), 0), order):
        place = pl.ds(pl.multiple_of((2 * i + par) * part, part), part)
        arrived(yr.at[i], y_s.at[i], y_r.at[i])
        y[place, :] = y[place, :] + yr[i]
        if step:
            send(y.at[place], zr.at[step - 1], z_s.at[step - 1], z_r.at[step - 1], r, 2 * i + par)

    for step in range(1, group):
        source = base + lax.rem(member + group - step, group)
        arrived(grp.at[source - base], g_s.at[step - 1], g_r.at[step - 1])
    for i in range(group):
        mt[i * width:(i + 1) * width, :] = grp[i].T
    mt_split = split(mt[...])

    total = y[pl.ds(pl.multiple_of(c * part, part), part), :]
    for step in range(1, half):
        arrived(zr.at[step - 1], z_s.at[step - 1], z_r.at[step - 1])
        total = total + zr[step - 1]
    for j in range(SIBS):
        block = -(my_place[0][j] * total[:, :NB] + my_place[1][j] * total[:, NB:])
        for i in range(group):
            stage[j * group + i] = block[:, i * width:(i + 1) * width]

    for step in range(1, C):
        to = lax.rem(c + step, C)
        send(stage.at[to], u.at[c], u_s.at[step - 1], u_r.at[step - 1], r, to)
    u[c] = stage[c]
    for j in range(C):
        panel_ref[:, j * width:(j + 1) * width] = stage[j]
    for step in range(1, C):
        source = lax.rem(c + C - step, C)
        arrived(u.at[source], u_s.at[step - 1], u_r.at[step - 1])
    x = u[...].reshape(rows, width)

    d_ref[...] = dot3(mt_split, split(x))
    for step in range(1, R):
        to = lax.rem(r + step, R)
        piece = d_ref.at[pl.ds(pl.multiple_of(to * chunk, chunk), chunk)]
        send(piece, rr.at[step - 1], d_s.at[step - 1], d_r.at[step - 1], to, c)
    upper_ref[...] = x.T
    total = d_ref[pl.ds(pl.multiple_of(r * chunk, chunk), chunk), :]
    for step in range(1, R):
        arrived(rr.at[step - 1], d_s.at[step - 1], d_r.at[step - 1])
        total = total + rr[step - 1]
    place = c // 2
    eg[par, r, place] = total

    def spread(which, step, side, at, over_pair):
        block = eg.at[side, r, at]
        if over_pair:
            send(block, block, ey_s.at[step], ey_r.at[step], r, other_c)
        for to in range(1, pairs):
            send(block, block, ex_s.at[which, to, step], ex_r.at[which, to, step],
                 same_parity(r, pairs, to), c)
        send(block, block, ec_s.at[which, 0, step], ec_r.at[which, 0, step], other_r, c)

    def onward(which, step, side, at):
        for to in range(1, pairs):
            block = eg.at[side, same_parity(r, pairs, pairs - to), at]
            arrived(block, ex_s.at[which, to, step], ex_r.at[which, to, step])
            send(block, block, ec_s.at[which, to, step], ec_r.at[which, to, step], other_r, c)

    mine = eg.at[par, r, place]
    for step in range(half - 1, 0, -1):
        to = flip(place, step)
        send(mine, mine, ez_s.at[step - 1], ez_r.at[step - 1], r, 2 * to + par)
    spread(0, 0, par, place, True)
    events = [(0, 1), (1, 0)]
    for step in range(2, half):
        events += [(0, step), (1, step - 1)]
    events.append((1, half - 1))
    before = (0, 0)
    for which, step in events:
        at = flip(place, step)
        if which == 0:
            arrived(eg.at[par, r, at], ez_s.at[step - 1], ez_r.at[step - 1])
            spread(0, step, par, at, True)
        else:
            arrived(eg.at[1 - par, r, at], ey_s.at[step], ey_r.at[step])
            spread(1, step, 1 - par, at, False)
        side = par if before[0] == 0 else 1 - par
        onward(*before, side, flip(place, before[1]))
        before = (which, step)
    onward(*before, par if before[0] == 0 else 1 - par, flip(place, before[1]))
    loads[4].wait()

    def assemble(parity):
        for column in range(C):
            j, i = column // group, column % group
            lanes = slice(i * width, (i + 1) * width)
            for pair in range(pairs):
                k = 2 * pair + parity
                span = pl.ds(pl.multiple_of(k * chunk, chunk), chunk)
                diag_ref[j, span, lanes] = inv_ref[j, span, lanes] - eg[column % 2, k, column // 2]

    assemble(rpar)
    for which in range(2):
        side = par if which == 0 else 1 - par
        for step in range(half):
            for to in range(pairs):
                block = eg.at[side, same_parity(other_r, pairs, (pairs - to) % pairs), flip(place, step)]
                arrived(block, ec_s.at[which, to, step], ec_r.at[which, to, step])
    assemble(1 - rpar)

    for op in sends:
        op.wait_send()
    for dest, args, span in own:
        @pl.when(dest != c)
        def _():
            copy(*args).wait_send()


def shards(R, C, trailing, panels, diag_inv, ancestors, owner_map):
    rows, cols = trailing.shape
    width = panels.shape[1]
    ratio = rows // cols
    part = rows // C
    group = NB // width
    half = C // 2
    pairs = R // 2
    chunk = NB // R
    wide = SHARE * NB
    dma = pltpu.SemaphoreType.DMA
    sems = [dma((5,))]
    for shape in (
        (ratio, R), (C,), (max(group - 1, 1),), (max(group - 1, 1),),
        (pairs, SIBS), (pairs, SIBS), (max(pairs - 1, 1), SIBS), (max(pairs - 1, 1), SIBS),
        (half,), (half,), (half - 1,), (half - 1,), (C - 1,), (C - 1,),
        (R - 1,), (R - 1,), (half - 1,), (half - 1,), (half,), (half,),
        (2, pairs, half), (2, pairs, half), (2, pairs, half), (2, pairs, half),
    ):
        sems.append(dma(shape))
    vmem = pl.BlockSpec(memory_space=pltpu.VMEM)
    anywhere = pl.BlockSpec(memory_space=pl.ANY)
    return pl.pallas_call(
        functools.partial(kernel, R, C),
        out_shape=(
            jax.ShapeDtypeStruct((part, SIBS * NB), F32),
            jax.ShapeDtypeStruct((width, rows), F32),
            jax.ShapeDtypeStruct(diag_inv.shape, F32),
        ),
        in_specs=[anywhere] * 5,
        out_specs=(vmem, vmem, vmem),
        scratch_shapes=[
            pltpu.SMEM(ancestors.shape, jnp.int32),
            pltpu.SMEM(owner_map.shape, jnp.int32),
            pltpu.VMEM(trailing.shape, F32),
            pltpu.VMEM(diag_inv.shape, F32),
            pltpu.VMEM(trailing.shape, BF16),
            pltpu.VMEM(trailing.shape, BF16),
            pltpu.VMEM((R, C, cols // R, width), F32),
            pltpu.VMEM((group, rows, width), F32),
            pltpu.VMEM((NB, rows), F32),
            pltpu.VMEM((rows // NB, cols, wide), F32),
            pltpu.VMEM((rows, wide), F32),
            pltpu.VMEM((half, part, wide), F32),
            pltpu.VMEM((half - 1, part, wide), F32),
            pltpu.VMEM((C, part, width), F32),
            pltpu.VMEM((C, part, width), F32),
            pltpu.VMEM((NB, width), F32),
            pltpu.VMEM((R - 1, chunk, width), F32),
            pltpu.VMEM((2, R, half, chunk, width), F32),
            *sems,
        ],
        compiler_params=pltpu.CompilerParams(
            has_side_effects=True, vmem_limit_bytes=56 * 1024 * 1024, collective_id=0
        ),
    )(ancestors, owner_map, trailing, panels, diag_inv)


def solution(mesh):
    placed = (P("prow", "pcol"), P("prow", "pcol"), P(), P(), P())
    return jax.shard_map(
        functools.partial(shards, mesh.shape["prow"], mesh.shape["pcol"]),
        mesh=mesh,
        in_specs=placed,
        out_specs=(P(("prow", "pcol"), None), P("pcol", "prow"), P()),
        check_vma=False,
    )
```

```python
import functools

import jax
import jax.numpy as jnp
from jax import lax
from jax.experimental import pallas as pl
from jax.experimental.pallas import tpu as pltpu
from jax.sharding import PartitionSpec as P

NB = 256
SIBS = 4
SHARE = 2
F32 = jnp.float32
BF16 = jnp.bfloat16


def split(value):
    high = value.astype(BF16)
    return high, (value - high.astype(F32)).astype(BF16)


def dot3(a, b):
    a_high, a_low = a
    b_high, b_low = b
    dot = functools.partial(jnp.dot, preferred_element_type=F32)
    return dot(a_high, b_high) + (dot(a_high, b_low) + dot(a_low, b_high))


def kernel(
    R, C, an_hbm, om_hbm, t_hbm, p_ref, inv_hbm, panel_ref, upper_ref, diag_ref,
    an, om, t_ref, inv_ref, t_high, t_low,
    pg, grp, mt, b_ref, y, yr, zr, stage, u, d_ref, rr, eg,
    load, a1_s, a1_r, g_s, g_r, a2_s, a2_r, a2f_s, a2f_r, y_s, y_r, z_s, z_r,
    u_s, u_r, d_s, d_r, ez_s, ez_r, ey_s, ey_r, ex_s, ex_r, ec_s, ec_r,
):
    r = lax.axis_index("prow")
    c = lax.axis_index("pcol")
    rows, cols = t_ref.shape
    width = p_ref.shape[1]
    ratio = rows // cols
    quarter = cols // R
    part = rows // C
    group = NB // width
    half = C // 2
    pairs = R // 2
    chunk = NB // R
    par = lax.rem(c, 2)
    other_c = c + 1 - 2 * par
    rpar = lax.rem(r, 2)
    other_r = r + 1 - 2 * rpar
    sends = []

    def copy(src, dst, ssem, rsem, to_r, to_c):
        return pltpu.make_async_remote_copy(
            src_ref=src, dst_ref=dst, send_sem=ssem, recv_sem=rsem,
            device_id=(to_r, to_c), device_id_type=pl.DeviceIdType.MESH,
        )

    def send(*args):
        op = copy(*args)
        op.start()
        sends.append(op)

    def arrived(dst, ssem, rsem):
        copy(dst, dst, ssem, rsem, other_r, c).wait_recv()

    def flip(index, bits):
        bit = 1
        out = index
        while bit <= bits:
            if bits & bit:
                out = out + bit * (1 - 2 * lax.rem(index // bit, 2))
            bit *= 2
        return out

    def same_parity(index, count, step):
        return lax.rem(index // 2 + step, count) * 2 + lax.rem(index, 2)

    loads = [
        pltpu.make_async_copy(src, dst, load.at[n])
        for n, (src, dst) in enumerate(
            ((p_ref, grp.at[lax.rem(c, group)]), (an_hbm, an), (om_hbm, om), (t_hbm, t_ref),
             (inv_hbm, inv_ref))
        )
    ]
    for op in loads:
        op.start()

    barrier = pltpu.get_barrier_semaphore()

    @pl.loop(1, R * C)
    def _(step):
        peer = lax.rem(r * C + c + step, R * C)
        pl.semaphore_signal(
            barrier, inc=1, device_id=(peer // C, lax.rem(peer, C)),
            device_id_type=pl.DeviceIdType.MESH,
        )

    for op in loads[:4]:
        op.wait()
    t_high[...], t_low[...] = split(t_ref[...])
    pl.semaphore_wait(barrier, R * C - 1)

    own = []
    for step in [*range(1, R), 0]:
        k = lax.rem(r + step, R)
        for b in range(ratio):
            dest = r * ratio + b
            span = pl.ds(pl.multiple_of(b * cols + k * quarter, quarter), quarter)
            piece = p_ref.at[span]
            args = (piece, pg.at[k, c], a1_s.at[b, step], a1_r.at[c], k, dest)
            if step:
                send(*args)
            else:
                own.append((dest, args, span))
    base = (c // group) * group
    member = c - base
    for dest, args, span in own:
        @pl.when(dest != c)
        def _():
            copy(*args).start()
    for dest, args, span in own:
        @pl.when(dest == c)
        def _():
            pg[r, c] = grp[member, span, :]

    slots = [[om[an[j, a]] for a in range(an.shape[1])] for j in range(SIBS)]

    def members(s):
        found = []
        for j in range(SIBS):
            flag = jnp.int32(0)
            for slot in slots[j]:
                flag = flag | jnp.where(slot == s, 1, 0).astype(jnp.int32)
            found.append(flag)
        return found

    def places(s):
        flags, before = members(s), jnp.int32(0)
        out = [[] for _ in range(SHARE)]
        for flag in flags:
            for k in range(SHARE):
                out[k].append((flag * jnp.where(before == k, 1, 0).astype(jnp.int32)).astype(F32))
            before = before + flag
        return out

    row_blocks = rows // NB
    first = (c // 2) // (half // row_blocks)
    blocks = [flip(first, n) for n in range(row_blocks - 1, -1, -1)]
    row_places = [places(r * row_blocks + b) for b in blocks]
    my_place = places((r * rows + c * part) // NB)
    col_flags = [flag.astype(F32) for flag in members(c)]

    root = c // ratio
    for step in range(SIBS):
        j = lax.rem(c // group + step, SIBS)
        for i in range(group):
            source = j * group + i
            @pl.when(jnp.logical_not((root == r) & (source == c)))
            def _():
                arrived(pg.at[r, source], a1_s.at[0, 0], a1_r.at[source])
        block = pg.at[r, pl.ds(j * group, group)]
        for to in range(1, pairs):
            send(block, block, a2_s.at[to, step], a2_r.at[to, j], same_parity(r, pairs, to), c)
        send(block, block, a2_s.at[0, step], a2_r.at[0, j], other_r, c)
    for step in range(1, group):
        to = base + lax.rem(member + step, group)
        send(p_ref, grp.at[member], g_s.at[step - 1], g_r.at[step - 1], r, to)
    for step in range(SIBS):
        for to in range(1, pairs):
            j = lax.rem(c // group + step, SIBS)
            source = same_parity(r, pairs, pairs - to)
            block = pg.at[source, pl.ds(j * group, group)]
            arrived(block, a2_s.at[to, step], a2_r.at[to, j])
            send(block, block, a2f_s.at[to - 1, step], a2f_r.at[to - 1, j], other_r, c)
    for j in range(SIBS):
        arrived(pg.at[other_r, pl.ds(j * group, group)], a2_s.at[0, j], a2_r.at[0, j])
        for to in range(1, pairs):
            source = same_parity(other_r, pairs, pairs - to)
            block = pg.at[source, pl.ds(j * group, group)]
            arrived(block, a2f_s.at[to - 1, j], a2f_r.at[to - 1, j])

    order = [flip(c // 2, step) for step in (*range(half - 1, 0, -1), 0)]
    for s in range(row_blocks):
        for k in range(SHARE):
            scale = [row_places[s][k][j] * col_flags[j] for j in range(SIBS)]
            for q in range(R):
                for i in range(group):
                    total = scale[0] * pg[q, i]
                    for j in range(1, SIBS):
                        total = total + scale[j] * pg[q, j * group + i]
                    b_ref[s, q * quarter:(q + 1) * quarter,
                          k * NB + i * width:k * NB + (i + 1) * width] = total
        here = pl.ds(pl.multiple_of(blocks[s] * NB, NB), NB)
        y[here, :] = dot3((t_high[here, :], t_low[here, :]), split(b_ref[s]))
        each = half // row_blocks
        for i in order[s * each:(s + 1) * each]:
            piece = y.at[pl.ds(pl.multiple_of((2 * i + 1 - par) * part, part), part)]
            send(piece, yr.at[i], y_s.at[i], y_r.at[i], r, other_c)
    levels = C.bit_length() - 1

    def landing(level, slot):
        if level == 0:
            i = flip(c // 2, slot)
            return yr.at[i], y_s.at[i], y_r.at[i]
        at = half - (half >> (level - 1)) + slot
        return zr.at[at], z_s.at[at], z_r.at[at]

    def summed(away, level):
        place = pl.ds(pl.multiple_of(flip(c, away) * part, part), part)
        total = y[place, :]
        for n in range(level):
            got = landing(n, away >> (n + 1))
            arrived(*got)
            total = total + got[0][...]
        return place, total

    for away in range(C - 2, 0, -2):
        level = (away & -away).bit_length() - 1
        place, total = summed(away, level)
        y[place, :] = total
        send(y.at[place], *landing(level, away >> (level + 1)), r, flip(c, 1 << level))

    for step in range(1, group):
        source = base + lax.rem(member + group - step, group)
        arrived(grp.at[source - base], g_s.at[step - 1], g_r.at[step - 1])
    for i in range(group):
        mt[i * width:(i + 1) * width, :] = grp[i].T
    mt_split = split(mt[...])

    _, total = summed(0, levels)
    for j in range(SIBS):
        block = -(my_place[0][j] * total[:, :NB] + my_place[1][j] * total[:, NB:])
        for i in range(group):
            stage[j * group + i] = block[:, i * width:(i + 1) * width]

    for step in range(1, C):
        to = lax.rem(c + step, C)
        send(stage.at[to], u.at[c], u_s.at[step - 1], u_r.at[step - 1], r, to)
    u[c] = stage[c]
    for j in range(C):
        panel_ref[:, j * width:(j + 1) * width] = stage[j]
    for step in range(1, C):
        source = lax.rem(c + C - step, C)
        arrived(u.at[source], u_s.at[step - 1], u_r.at[step - 1])
    x = u[...].reshape(rows, width)

    d_ref[...] = dot3(mt_split, split(x))
    for step in range(1, R):
        to = lax.rem(r + step, R)
        piece = d_ref.at[pl.ds(pl.multiple_of(to * chunk, chunk), chunk)]
        send(piece, rr.at[step - 1], d_s.at[step - 1], d_r.at[step - 1], to, c)
    upper_ref[...] = x.T
    total = d_ref[pl.ds(pl.multiple_of(r * chunk, chunk), chunk), :]
    for step in range(1, R):
        arrived(rr.at[step - 1], d_s.at[step - 1], d_r.at[step - 1])
        total = total + rr[step - 1]
    place = c // 2
    eg[par, r, place] = total

    def spread(which, step, side, at, over_pair):
        block = eg.at[side, r, at]
        if over_pair:
            send(block, block, ey_s.at[step], ey_r.at[step], r, other_c)
        for to in range(1, pairs):
            send(block, block, ex_s.at[which, to, step], ex_r.at[which, to, step],
                 same_parity(r, pairs, to), c)
        send(block, block, ec_s.at[which, 0, step], ec_r.at[which, 0, step], other_r, c)

    def onward(which, step, side, at):
        for to in range(1, pairs):
            block = eg.at[side, same_parity(r, pairs, pairs - to), at]
            arrived(block, ex_s.at[which, to, step], ex_r.at[which, to, step])
            send(block, block, ec_s.at[which, to, step], ec_r.at[which, to, step], other_r, c)

    mine = eg.at[par, r, place]
    for step in range(half - 1, 0, -1):
        to = flip(place, step)
        send(mine, mine, ez_s.at[step - 1], ez_r.at[step - 1], r, 2 * to + par)
    spread(0, 0, par, place, True)
    events = [(0, 1), (1, 0)]
    for step in range(2, half):
        events += [(0, step), (1, step - 1)]
    events.append((1, half - 1))
    before = (0, 0)
    for which, step in events:
        at = flip(place, step)
        if which == 0:
            arrived(eg.at[par, r, at], ez_s.at[step - 1], ez_r.at[step - 1])
            spread(0, step, par, at, True)
        else:
            arrived(eg.at[1 - par, r, at], ey_s.at[step], ey_r.at[step])
            spread(1, step, 1 - par, at, False)
        side = par if before[0] == 0 else 1 - par
        onward(*before, side, flip(place, before[1]))
        before = (which, step)
    onward(*before, par if before[0] == 0 else 1 - par, flip(place, before[1]))
    loads[4].wait()

    def assemble(parity):
        for column in range(C):
            j, i = column // group, column % group
            lanes = slice(i * width, (i + 1) * width)
            for pair in range(pairs):
                k = 2 * pair + parity
                span = pl.ds(pl.multiple_of(k * chunk, chunk), chunk)
                diag_ref[j, span, lanes] = inv_ref[j, span, lanes] - eg[column % 2, k, column // 2]

    assemble(rpar)
    for which in range(2):
        side = par if which == 0 else 1 - par
        for step in range(half):
            for to in range(pairs):
                block = eg.at[side, same_parity(other_r, pairs, (pairs - to) % pairs), flip(place, step)]
                arrived(block, ec_s.at[which, to, step], ec_r.at[which, to, step])
    assemble(1 - rpar)

    for op in sends:
        op.wait_send()
    for dest, args, span in own:
        @pl.when(dest != c)
        def _():
            copy(*args).wait_send()


def shards(R, C, trailing, panels, diag_inv, ancestors, owner_map):
    rows, cols = trailing.shape
    width = panels.shape[1]
    ratio = rows // cols
    part = rows // C
    group = NB // width
    half = C // 2
    pairs = R // 2
    chunk = NB // R
    wide = SHARE * NB
    dma = pltpu.SemaphoreType.DMA
    sems = [dma((5,))]
    for shape in (
        (ratio, R), (C,), (max(group - 1, 1),), (max(group - 1, 1),),
        (pairs, SIBS), (pairs, SIBS), (max(pairs - 1, 1), SIBS), (max(pairs - 1, 1), SIBS),
        (half,), (half,), (half - 1,), (half - 1,), (C - 1,), (C - 1,),
        (R - 1,), (R - 1,), (half - 1,), (half - 1,), (half,), (half,),
        (2, pairs, half), (2, pairs, half), (2, pairs, half), (2, pairs, half),
    ):
        sems.append(dma(shape))
    vmem = pl.BlockSpec(memory_space=pltpu.VMEM)
    anywhere = pl.BlockSpec(memory_space=pl.ANY)
    return pl.pallas_call(
        functools.partial(kernel, R, C),
        out_shape=(
            jax.ShapeDtypeStruct((part, SIBS * NB), F32),
            jax.ShapeDtypeStruct((width, rows), F32),
            jax.ShapeDtypeStruct(diag_inv.shape, F32),
        ),
        in_specs=[anywhere] * 5,
        out_specs=(vmem, vmem, vmem),
        scratch_shapes=[
            pltpu.SMEM(ancestors.shape, jnp.int32),
            pltpu.SMEM(owner_map.shape, jnp.int32),
            pltpu.VMEM(trailing.shape, F32),
            pltpu.VMEM(diag_inv.shape, F32),
            pltpu.VMEM(trailing.shape, BF16),
            pltpu.VMEM(trailing.shape, BF16),
            pltpu.VMEM((R, C, cols // R, width), F32),
            pltpu.VMEM((group, rows, width), F32),
            pltpu.VMEM((NB, rows), F32),
            pltpu.VMEM((rows // NB, cols, wide), F32),
            pltpu.VMEM((rows, wide), F32),
            pltpu.VMEM((half, part, wide), F32),
            pltpu.VMEM((half - 1, part, wide), F32),
            pltpu.VMEM((C, part, width), F32),
            pltpu.VMEM((C, part, width), F32),
            pltpu.VMEM((NB, width), F32),
            pltpu.VMEM((R - 1, chunk, width), F32),
            pltpu.VMEM((2, R, half, chunk, width), F32),
            *sems,
        ],
        compiler_params=pltpu.CompilerParams(
            has_side_effects=True, vmem_limit_bytes=56 * 1024 * 1024, collective_id=0
        ),
    )(ancestors, owner_map, trailing, panels, diag_inv)


def solution(mesh):
    placed = (P("prow", "pcol"), P("prow", "pcol"), P(), P(), P())
    return jax.shard_map(
        functools.partial(shards, mesh.shape["prow"], mesh.shape["pcol"]),
        mesh=mesh,
        in_specs=placed,
        out_specs=(P(("prow", "pcol"), None), P("pcol", "prow"), P()),
        check_vma=False,
    )
```
